32 devices in a mesh: dp: 16 (over z, y, x), tensor: 2 (over core).
Axes of the slice: x: 2, y: 2, z: 4, core: 2. Of those that a mesh axis runs over, the one named last changes fastest.
Arguments:
- fc_grads: bfloat16 [16, 768, 3072], P('dp', None, 'tensor')
- fc_error: bfloat16 [16, 768, 3072], P('dp', None, 'tensor'), may hold values from -4 to 4
- query: float32 [3072, 32], P('tensor'), may hold values from -0.109375 to 0.109375
- gram_inverse: float32 [32, 32], replicated
- fc_master: float32 [768, 3072], P('dp', 'tensor'), may hold values from -6 to 6
- fc_momentum: float32 [768, 3072], P('dp', 'tensor'), may hold values from -3 to 3
- vec_grads: bfloat16 [16, 5376], P('dp'), may hold values from -6 to 6
- vec_master: float32 [5376], P('dp'), may hold values from -6 to 6
- vec_momentum: float32 [5376], P('dp'), may hold values from -4 to 4
Outputs:
- new_error: bfloat16 [16, 768, 3072], P('dp', None, 'tensor')
- new_momentum: float32 [768, 3072], P('dp', 'tensor')
- new_master: float32 [768, 3072], P('dp', 'tensor')
- new_weights: bfloat16 [768, 3072], P(None, 'tensor')
- vec_new_momentum: float32 [5376], P('dp')
- vec_new_master: float32 [5376], P('dp')
- vec_weights: bfloat16 [5376], replicated
The draws below stay inside these ranges and needn't reach their ends.
All inputs are finite; a program needn't handle non-finite values.
Results may differ from the reference program's by a relative error of at most 0.0085.
Values may be sent and summed in bfloat16 or wider, within the bound.
A program may use at most 64 MiB of HBM per device.

```python
import jax
import jax.numpy as jnp
from jax import lax

D = 768
FF = 3072
RANK = 32
REPLICAS = 16
VEC = 5376
N_DP = 16


def draw_fc_grads(key, part):
    common_key = jax.random.fold_in(key, 11)
    noise_key = jax.random.fold_in(key, 12)
    common = 0.2 * jax.random.normal(common_key, (D, FF), jnp.float32)
    noise = jax.random.normal(noise_key, (REPLICAS, D, FF), jnp.float32)
    return (common + noise).astype(jnp.bfloat16)


def draw_gram_inverse(key, part):
    diag_key = jax.random.fold_in(key, 21)
    off_key = jax.random.fold_in(key, 22)
    bound = 0.78 / (RANK - 1)
    diag_values = jax.random.uniform(diag_key, (RANK,), jnp.float32, 0.8, 1.2)
    off_values = jax.random.uniform(off_key, (RANK, RANK), jnp.float32, -bound, bound)
    eye_mask = jnp.eye(RANK, dtype=jnp.float32)
    matrix = off_values * (1.0 - eye_mask) + eye_mask * diag_values[None, :]
    return matrix * (10.0 * D ** (-0.5))


def raised(values, rng, source, target, parts, factor):
    owner, partner = [(jnp.arange(values.shape[dim]) // (values.shape[dim] // parts)).reshape([-1 if axis == dim else 1 for axis in range(values.ndim)]) for dim in (source, target)]
    chosen = jax.random.permutation(rng, parts)[partner]
    strong = (owner == chosen) | (owner == (partner + parts // 2) % parts)
    return jnp.where(strong, factor * values, values)


def shard_levels(own_key, dims, cuts, low, top_value):
    def one(axis_at, parts):
        steps = jax.random.uniform(jax.random.fold_in(jax.random.fold_in(own_key, 6), axis_at), (parts,), jnp.float32, low / len(cuts), top_value / len(cuts))
        return jnp.repeat(jnp.exp(steps), dims[axis_at] // parts).reshape((-1,) + (1,) * (len(dims) - axis_at - 1))

    loudness = one(*cuts[0])
    for cut in cuts[1:]:
        loudness = loudness * one(*cut)
    return loudness


def scatter_about(rng, shape, deviation, most, shards=(), held_as=jnp.bfloat16):
    entries = jax.random.normal(rng, shape, jnp.float32) * deviation
    if len(shards) > 0:
        entries = shard_levels(rng, shape, shards, -0.22, 0.18) * entries
    return jnp.clip(entries, min=-most, max=most).astype(held_as)


def bell_draw_with(key, dims, deviation, most, pieces, heavy, held_as=jnp.bfloat16):
    entries = deviation * jax.random.normal(key, dims, jnp.float32)
    if pieces:
        entries = entries * shard_levels(key, dims, pieces, -0.22, 0.18)
    return jnp.clip(raised(entries, jax.random.fold_in(key, 3), *heavy), -most, most).astype(held_as)


def setup_inputs(seed: int = 0) -> dict:
    arg_keys = jax.random.split(jax.random.key(seed), 10)
    return {
        "fc_grads": draw_fc_grads(jax.random.fold_in(arg_keys[9], 71), 0),
        "fc_error": scatter_about(arg_keys[1], (REPLICAS, D, FF), 0.3, 4.0, ((0, 16), (2, 2))),
        "query": scatter_about(arg_keys[2], (FF, RANK), FF ** -0.5, 0.109375, ((0, 2),), jnp.float32),
        "gram_inverse": draw_gram_inverse(jax.random.fold_in(arg_keys[9], 71), 0),
        "fc_master": scatter_about(arg_keys[4], (D, FF), 0.5, 6.0, ((0, 16), (1, 2)), jnp.float32),
        "fc_momentum": scatter_about(arg_keys[5], (D, FF), 0.2, 3.0, ((0, 16), (1, 2)), jnp.float32),
        "vec_grads": bell_draw_with(arg_keys[6], (REPLICAS, VEC), 1.0, 6.0, ((0, 16),), (0, 1, 16, 2.0)),
        "vec_master": scatter_about(arg_keys[7], (VEC,), 0.5, 6.0, ((0, 16),), jnp.float32),
        "vec_momentum": scatter_about(arg_keys[8], (VEC,), 0.3, 4.0, ((0, 16),), jnp.float32),
    }


momentum_decay = 0.9
step_size = 0.5


def combine(grad_piece, error_piece):
    return (grad_piece.astype(jnp.float32) + error_piece.astype(jnp.float32)).astype(jnp.bfloat16)


def reference(fc_grads, fc_error, query, gram_inverse, fc_master, fc_momentum, vec_grads, vec_master, vec_momentum):
    query_b = query.astype(jnp.bfloat16)

    def row_step(total, pair):
        merged = combine(pair[0], pair[1])
        return total + jnp.dot(merged, query_b, preferred_element_type=jnp.float32), None

    row_total, unused = lax.scan(row_step, jnp.zeros((D, RANK), jnp.float32), (fc_grads, fc_error))
    row_mean = row_total / N_DP
    row_basis = jnp.dot(row_mean, gram_inverse, precision=lax.Precision.HIGHEST)
    basis_b = row_basis.astype(jnp.bfloat16)

    def col_step(total, pair):
        merged = combine(pair[0], pair[1])
        term = lax.dot_general(merged, basis_b, (((0,), (0,)), ((), ())), preferred_element_type=jnp.float32)
        return total + term, None

    col_total, unused = lax.scan(col_step, jnp.zeros((FF, RANK), jnp.float32), (fc_grads, fc_error))
    col_mean = col_total / N_DP
    approx = jnp.dot(row_basis, col_mean.T, precision=lax.Precision.HIGHEST)

    def error_step(pair):
        merged = lax.optimization_barrier(combine(pair[0], pair[1]))
        return (merged.astype(jnp.float32) - approx).astype(jnp.bfloat16)

    new_error = lax.map(error_step, (fc_grads, fc_error))
    new_momentum = momentum_decay * fc_momentum + approx
    new_master = fc_master - step_size * (approx + momentum_decay * new_momentum)
    new_weights = new_master.astype(jnp.bfloat16)
    vec_mean = jnp.sum(vec_grads.astype(jnp.float32), axis=0) / N_DP
    vec_new_momentum = momentum_decay * vec_momentum + vec_mean
    vec_new_master = vec_master - step_size * (vec_mean + momentum_decay * vec_new_momentum)
    vec_weights = vec_new_master.astype(jnp.bfloat16)
    return (new_error, new_momentum, new_master, new_weights, vec_new_momentum, vec_new_master, vec_weights)
```

```python
import functools

import jax
import jax.numpy as jnp
from jax import lax
from jax.experimental import pallas as pl
from jax.experimental.pallas import tpu as pltpu
from jax.sharding import PartitionSpec as P

momentum_decay = 0.9
step_size = 0.5
base_decay = step_size * momentum_decay * momentum_decay
approx_scale = step_size * (1.0 + momentum_decay)

MESH = pl.DeviceIdType.MESH
INNER = 4
ROW_BLOCK = 128
COL_OWNERS = 16
VMEM_LIMIT = 40 * 1024 * 1024


def remote(src, dst, send_sem, recv_sem, dp, core):
    return pltpu.make_async_remote_copy(
        src_ref=src,
        dst_ref=dst,
        send_sem=send_sem,
        recv_sem=recv_sem,
        device_id=(dp, core),
        device_id_type=MESH,
    )


def wait_bytes(ref, sem):
    pltpu.make_async_copy(ref, ref, sem).wait()


def exchange_kernel(
    n,
    cores,
    grads,
    error,
    query,
    gram,
    vec_in,
    master,
    momentum,
    merged_out,
    base_all,
    basis_out,
    col_out,
    vec_out,
    grads_v,
    error_v,
    merged,
    own_base,
    part,
    part_in,
    total,
    col_part,
    col_in,
    col_total,
    load_sem,
    out_sem,
    part_send,
    part_recv,
    total_send,
    total_recv,
    cpart_send,
    cpart_recv,
    ctotal_send,
    ctotal_recv,
    base_send,
    line_recv,
    plane_recv,
):
    rows_all, columns = merged.shape
    blocks = rows_all // ROW_BLOCK
    row_chunks = 2 * blocks
    chunks = part.shape[0]
    devices = n * cores
    me, core = lax.axis_index("dp"), lax.axis_index("tensor")
    flat = core * n + me
    outer = n // INNER
    o, i = lax.div(me, INNER), lax.rem(me, INNER)

    def load(b):
        rows = pl.ds(pl.multiple_of(b * ROW_BLOCK, ROW_BLOCK), ROW_BLOCK)
        return (
            pltpu.make_async_copy(grads.at[0, rows], grads_v.at[rows], load_sem.at[b, 0]),
            pltpu.make_async_copy(error.at[0, rows], error_v.at[rows], load_sem.at[b, 1]),
        )

    for b in range(blocks):
        for copy in load(b):
            copy.start()

    barrier = pltpu.get_barrier_semaphore()

    def greet(t, carry):
        f = lax.rem(flat + t, devices)
        pl.semaphore_signal(
            barrier, inc=1, device_id=(lax.rem(f, n), lax.div(f, n)), device_id_type=MESH
        )
        return carry

    lax.fori_loop(1, devices, greet, 0)

    own_base[...] = (master[...] - base_decay * momentum[...]).astype(jnp.bfloat16)
    query_t = query[...].T.astype(jnp.bfloat16)
    part[row_chunks:] = vec_in[...]

    pl.semaphore_wait(barrier, devices - 1)

    keep = pltpu.make_async_copy(own_base, base_all.at[me], out_sem.at[0])
    keep.start()

    def send_line(t, carry):
        o2 = lax.rem(o + t, outer)
        remote(
            own_base, base_all.at[me], base_send, line_recv.at[o], o2 * INNER + i, core
        ).start()
        return carry

    lax.fori_loop(1, outer, send_line, 0)

    def send_plane(s, carry):
        i2 = lax.rem(i + s, INNER)
        remote(own_base, base_all.at[me], base_send, plane_recv, o * INNER + i2, core).start()
        return carry

    lax.fori_loop(1, INNER, send_plane, 0)

    def send_part(k):
        mine = flat == k

        @pl.when(mine)
        def _():
            part_in[pl.ds(flat, 1)] = part[pl.ds(k, 1)]

        @pl.when(jnp.logical_not(mine))
        def _():
            remote(
                part.at[k], part_in.at[flat], part_send, part_recv, lax.rem(k, n), lax.div(k, n)
            ).start()

    def send_vec(k, carry):
        send_part(k)
        return carry

    lax.fori_loop(row_chunks, chunks, send_vec, 0)

    def row_step(b, carry):
        for copy in load(b):
            copy.wait()
        rows = pl.ds(pl.multiple_of(b * ROW_BLOCK, ROW_BLOCK), ROW_BLOCK)
        block = (
            grads_v[rows, :].astype(jnp.float32) + error_v[rows, :].astype(jnp.float32)
        ).astype(jnp.bfloat16)
        merged[rows, :] = block
        term = lax.dot_general(
            query_t, block, (((1,), (1,)), ((), ())), preferred_element_type=jnp.float32
        )
        part[pl.ds(2 * b, 1)] = term[None, :16]
        part[pl.ds(2 * b + 1, 1)] = term[None, 16:]
        send_part(2 * b)
        send_part(2 * b + 1)
        return carry

    lax.fori_loop(0, blocks, row_step, 0)
    keep_merged = pltpu.make_async_copy(merged, merged_out, out_sem.at[1])
    keep_merged.start()

    owner = flat < chunks

    @pl.when(owner)
    def _():
        wait_bytes(part_in.at[pl.ds(0, devices - 1)], part_recv)
        total[pl.ds(flat, 1)] = jnp.sum(part_in[...], axis=0)[None]

        def spread(t, carry):
            f = lax.rem(flat + t, devices)
            remote(
                total.at[flat],
                total.at[flat],
                total_send,
                total_recv,
                lax.rem(f, n),
                lax.div(f, n),
            ).start()
            return carry

        lax.fori_loop(1, devices, spread, 0)
        wait_bytes(total.at[pl.ds(0, chunks - 1)], total_recv)

    @pl.when(jnp.logical_not(owner))
    def _():
        wait_bytes(total.at[pl.ds(0, chunks)], total_recv)

    row_mean = (
        jnp.concatenate(
            [
                jnp.concatenate([total[2 * b], total[2 * b + 1]], axis=0)
                for b in range(blocks)
            ],
            axis=1,
        )
        / n
    )
    basis = jnp.dot(
        gram[...].T,
        row_mean,
        precision=lax.Precision.HIGHEST,
        preferred_element_type=jnp.float32,
    )
    basis_b = basis.astype(jnp.bfloat16)

    wide = columns // 4
    for c in range(4):
        term = jnp.dot(
            basis_b, merged[:, c * wide : (c + 1) * wide], preferred_element_type=jnp.float32
        )
        for r in range(4):
            k = 4 * c + r
            col_part[k] = term[8 * r : 8 * r + 8]
        for r in range(4):
            k = 4 * c + r

            @pl.when(me == k)
            def _(k=k):
                col_in[pl.ds(me, 1)] = col_part[pl.ds(k, 1)]

            @pl.when(me != k)
            def _(k=k):
                remote(
                    col_part.at[k], col_in.at[me], cpart_send, cpart_recv, k, core
                ).start()

    def relay(t, carry):
        o2 = lax.rem(o + outer - t, outer)
        slot = o2 * INNER + i
        wait_bytes(base_all.at[slot], line_recv.at[o2])

        def hand(s, inner_carry):
            i2 = lax.rem(i + s, INNER)
            remote(
                base_all.at[slot],
                base_all.at[slot],
                base_send,
                plane_recv,
                o * INNER + i2,
                core,
            ).start()
            return inner_carry

        return lax.fori_loop(1, INNER, hand, carry)

    lax.fori_loop(1, outer, relay, 0)

    high = basis_b.astype(jnp.float32)
    low = basis - high
    basis_out[...] = jnp.concatenate([high, low, high, low], axis=0).T.astype(jnp.bfloat16)
    vec_out[...] = total[row_chunks:]

    def col_owner():
        wait_bytes(col_in.at[pl.ds(0, n - 1)], cpart_recv)
        col_total[pl.ds(me, 1)] = jnp.sum(col_in[...], axis=0)[None]

        def spread(t, carry):
            remote(
                col_total.at[me],
                col_total.at[me],
                ctotal_send,
                ctotal_recv,
                lax.rem(me + t, n),
                core,
            ).start()
            return carry

        lax.fori_loop(1, n, spread, 0)
        wait_bytes(col_total.at[pl.ds(0, COL_OWNERS - 1)], ctotal_recv)

    if n == COL_OWNERS:
        col_owner()
    else:
        pl.when(me < COL_OWNERS)(col_owner)

        @pl.when(me >= COL_OWNERS)
        def _():
            wait_bytes(col_total.at[pl.ds(0, COL_OWNERS)], ctotal_recv)

    for c in range(4):
        col_mean = jnp.concatenate([col_total[4 * c + r] for r in range(4)], axis=0) / n
        col_high = col_mean.astype(jnp.bfloat16)
        col_low = (col_mean - col_high.astype(jnp.float32)).astype(jnp.bfloat16)
        col_out[:, c * wide : (c + 1) * wide] = jnp.concatenate(
            [col_high, col_high, col_low, col_low], axis=0
        )

    keep.wait()
    keep_merged.wait()

    @pl.when(owner)
    def _():
        wait_bytes(part.at[pl.ds(0, chunks - 1)], part_send)
        wait_bytes(part_in.at[pl.ds(0, devices - 1)], total_send)

    @pl.when(jnp.logical_not(owner))
    def _():
        wait_bytes(part.at[pl.ds(0, chunks)], part_send)

    def col_sent():
        wait_bytes(col_part.at[pl.ds(0, COL_OWNERS - 1)], cpart_send)
        wait_bytes(col_in.at[pl.ds(0, n - 1)], ctotal_send)

    if n == COL_OWNERS:
        col_sent()
    else:
        pl.when(me < COL_OWNERS)(col_sent)

        @pl.when(me >= COL_OWNERS)
        def _():
            wait_bytes(col_part.at[pl.ds(0, COL_OWNERS)], cpart_send)

    wait_bytes(base_all.at[pl.ds(0, (INNER - 1) * outer)], plane_recv)
    wait_bytes(base_all.at[pl.ds(0, n - 1)], base_send)


def exchange(n, cores, grads, error, query, gram, vec_in, master, momentum):
    rows_all, columns = grads.shape[1:]
    rank = query.shape[1]
    rows = master.shape[0]
    blocks = rows_all // ROW_BLOCK
    chunks = 2 * blocks + vec_in.shape[0]
    wide = columns // 4
    devices = n * cores
    vmem = pl.BlockSpec(memory_space=pltpu.VMEM)
    hbm = pl.BlockSpec(memory_space=pl.ANY)
    dma = pltpu.SemaphoreType.DMA
    f32, bf16 = jnp.float32, jnp.bfloat16
    return pl.pallas_call(
        functools.partial(exchange_kernel, n, cores),
        out_shape=(
            jax.ShapeDtypeStruct((rows_all, columns), bf16),
            jax.ShapeDtypeStruct((n, rows, columns), bf16),
            jax.ShapeDtypeStruct((rows_all, 4 * rank), bf16),
            jax.ShapeDtypeStruct((4 * rank, columns), bf16),
            jax.ShapeDtypeStruct(vec_in.shape, f32),
        ),
        in_specs=[hbm, hbm, vmem, vmem, vmem, vmem, vmem],
        out_specs=(hbm, hbm, vmem, vmem, vmem),
        scratch_shapes=[
            pltpu.VMEM((rows_all, columns), bf16),
            pltpu.VMEM((rows_all, columns), bf16),
            pltpu.VMEM((rows_all, columns), bf16),
            pltpu.VMEM((rows, columns), bf16),
            pltpu.VMEM((chunks, 16, 128), f32),
            pltpu.VMEM((devices, 16, 128), f32),
            pltpu.VMEM((chunks, 16, 128), f32),
            pltpu.VMEM((COL_OWNERS, 8, wide), f32),
            pltpu.VMEM((n, 8, wide), f32),
            pltpu.VMEM((COL_OWNERS, 8, wide), f32),
            dma((blocks, 2)),
            dma((2,)),
        ]
        + [dma] * 8
        + [dma, dma((n // INNER,)), dma],
        compiler_params=pltpu.CompilerParams(
            collective_id=0, has_side_effects=True, vmem_limit_bytes=VMEM_LIMIT
        ),
        cost_estimate=pl.CostEstimate(
            flops=4 * rows_all * columns * rank, bytes_accessed=14000000, transcendentals=0
        ),
        name="exchange",
    )(grads, error, query, gram, vec_in, master, momentum)


def update_kernel(
    rows_step,
    merged,
    base,
    basis,
    col,
    master,
    momentum,
    new_error,
    new_momentum,
    new_master,
    new_weights,
):
    step = pl.program_id(0)
    here = pl.ds(pl.multiple_of(step * rows_step, rows_step), rows_step)
    approx = jnp.dot(basis[here, :], col[...], preferred_element_type=jnp.float32)
    new_error[...] = (merged[...].astype(jnp.float32) - approx).astype(jnp.bfloat16)
    new_weights[...] = (base[...].astype(jnp.float32) - approx_scale * approx).astype(
        jnp.bfloat16
    )

    @pl.when(step == 0)
    def _():
        rows, rows_all = master.shape[0], basis.shape[0]
        first = lax.axis_index("dp") * rows
        shape = (rows, rows_all)
        chosen = lax.broadcasted_iota(jnp.int32, shape, 1) == first + lax.broadcasted_iota(
            jnp.int32, shape, 0
        )
        basis_rows = jnp.dot(
            chosen.astype(jnp.float32).astype(jnp.bfloat16),
            basis[...],
            preferred_element_type=jnp.float32,
        ).astype(jnp.bfloat16)
        approx_rows = jnp.dot(basis_rows, col[...], preferred_element_type=jnp.float32)
        moved = momentum_decay * momentum[...] + approx_rows
        new_momentum[...] = moved
        new_master[...] = master[...] - step_size * (approx_rows + momentum_decay * moved)


def update(merged, base, basis, col, master, momentum):
    rows_all, columns = merged.shape
    steps = 6
    rows_step = rows_all // steps
    tile = pl.BlockSpec((rows_step, columns), lambda s: (s, 0))

    def whole(x):
        return pl.BlockSpec(x.shape, lambda s: (0, 0))

    state = jax.ShapeDtypeStruct(master.shape, jnp.float32)
    return pl.pallas_call(
        functools.partial(update_kernel, rows_step),
        grid=(steps,),
        out_shape=(
            jax.ShapeDtypeStruct((1, rows_all, columns), jnp.bfloat16),
            state,
            state,
            jax.ShapeDtypeStruct((rows_all, columns), jnp.bfloat16),
        ),
        in_specs=[tile, tile, whole(basis), whole(col), whole(master), whole(momentum)],
        out_specs=(
            pl.BlockSpec((None, rows_step, columns), lambda s: (0, s, 0)),
            whole(master),
            whole(master),
            tile,
        ),
        compiler_params=pltpu.CompilerParams(vmem_limit_bytes=VMEM_LIMIT),
        name="update",
    )(merged, base, basis, col, master, momentum)


def on_device(
    n,
    cores,
    fc_grads,
    fc_error,
    query,
    gram_inverse,
    fc_master,
    fc_momentum,
    vec_grads,
    vec_master,
    vec_momentum,
):
    replica = lax.axis_index("dp")
    length, shard = vec_grads.shape[1], vec_master.shape[0]
    counts = (lax.axis_index("tensor") == 0).astype(jnp.float32)
    padded = -(-length // 2048) * 2048
    vec_base = lax.dynamic_update_slice_in_dim(
        jnp.zeros((padded,), jnp.float32),
        vec_master - base_decay * vec_momentum,
        replica * shard,
        0,
    )
    vec_sum = jnp.pad(vec_grads[0].astype(jnp.float32), (0, padded - length))
    vec_in = (counts * jnp.concatenate([vec_sum, vec_base])).reshape(-1, 16, 128)

    merged, base, basis, col, vec_out = exchange(
        n, cores, fc_grads, fc_error, query, gram_inverse, vec_in, fc_master, fc_momentum
    )
    new_error, new_momentum, new_master, new_weights = update(
        merged, base.reshape(merged.shape), basis, col, fc_master, fc_momentum
    )
    vec_out = vec_out.reshape(2, padded)
    vec_weights = (vec_out[1, :length] - approx_scale / n * vec_out[0, :length]).astype(
        jnp.bfloat16
    )
    vec_mean = lax.dynamic_slice_in_dim(vec_out[0], replica * shard, shard, 0) / n
    vec_new_momentum = momentum_decay * vec_momentum + vec_mean
    vec_new_master = vec_master - step_size * (vec_mean + momentum_decay * vec_new_momentum)
    return (
        new_error,
        new_momentum,
        new_master,
        new_weights,
        vec_new_momentum,
        vec_new_master,
        vec_weights,
    )


def solution(mesh):
    return jax.shard_map(
        functools.partial(on_device, mesh.shape["dp"], mesh.shape["tensor"]),
        mesh=mesh,
        in_specs=(
            P("dp", None, "tensor"),
            P("dp", None, "tensor"),
            P("tensor", None),
            P(),
            P("dp", "tensor"),
            P("dp", "tensor"),
            P("dp", None),
            P("dp"),
            P("dp"),
        ),
        out_specs=(
            P("dp", None, "tensor"),
            P("dp", "tensor"),
            P("dp", "tensor"),
            P(None, "tensor"),
            P("dp"),
            P("dp"),
            P(),
        ),
        check_vma=False,
    )
```

```python
import functools

import jax
import jax.numpy as jnp
from jax import lax
from jax.experimental import pallas as pl
from jax.experimental.pallas import tpu as pltpu
from jax.sharding import PartitionSpec as P

momentum_decay = 0.9
step_size = 0.5
base_decay = step_size * momentum_decay * momentum_decay
approx_scale = step_size * (1.0 + momentum_decay)

MESH = pl.DeviceIdType.MESH
INNER = 4
ROW_BLOCK = 128
COL_OWNERS = 16
VMEM_LIMIT = 40 * 1024 * 1024


def remote(src, dst, send_sem, recv_sem, dp, core):
    return pltpu.make_async_remote_copy(
        src_ref=src,
        dst_ref=dst,
        send_sem=send_sem,
        recv_sem=recv_sem,
        device_id=(dp, core),
        device_id_type=MESH,
    )


def wait_bytes(ref, sem):
    pltpu.make_async_copy(ref, ref, sem).wait()


def exchange_kernel(
    n,
    cores,
    grads,
    error,
    query_t,
    gram,
    vec_grads,
    vec_base,
    master,
    momentum,
    merged_out,
    base_all,
    basis_out,
    col_out,
    vec_out,
    grads_v,
    error_v,
    query_v,
    gram_v,
    master_v,
    momentum_v,
    merged,
    own_base,
    part,
    part_in,
    total,
    col_part,
    col_in,
    col_total,
    load_sem,
    small_sem,
    out_sem,
    part_send,
    part_recv,
    total_send,
    total_recv,
    cpart_send,
    cpart_recv,
    ctotal_send,
    ctotal_recv,
    base_send,
    line_recv,
    x_recv,
    y_recv,
    corner_recv,
):
    rows_all, columns = merged.shape
    blocks = rows_all // ROW_BLOCK
    row_chunks = 2 * blocks
    chunks = part.shape[0]
    vec_chunks = (chunks - row_chunks) // 2
    devices = n * cores
    me, core = lax.axis_index("dp"), lax.axis_index("tensor")
    flat = core * n + me
    outer = n // INNER
    o, i = lax.div(me, INNER), lax.rem(me, INNER)
    ix = i + 1 - 2 * lax.rem(i, 2)
    iy = lax.rem(i + 2, INNER)

    small = [
        pltpu.make_async_copy(src, dst, small_sem.at[k])
        for k, (src, dst) in enumerate(
            ((master, master_v), (momentum, momentum_v), (query_t, query_v), (gram, gram_v))
        )
    ]
    for copy in small:
        copy.start()

    def load(b):
        rows = pl.ds(pl.multiple_of(b * ROW_BLOCK, ROW_BLOCK), ROW_BLOCK)
        return (
            pltpu.make_async_copy(grads.at[0, rows], grads_v.at[rows], load_sem.at[b, 0]),
            pltpu.make_async_copy(error.at[0, rows], error_v.at[rows], load_sem.at[b, 1]),
        )

    for b in range(blocks):
        for copy in load(b):
            copy.start()

    barrier = pltpu.get_barrier_semaphore()

    def greet(t, carry):
        f = lax.rem(flat + t, devices)
        pl.semaphore_signal(
            barrier, inc=1, device_id=(lax.rem(f, n), lax.div(f, n)), device_id_type=MESH
        )
        return carry

    lax.fori_loop(1, devices, greet, 0)

    vec = vec_grads[...].astype(jnp.float32) * (core == 0).astype(jnp.float32)
    lanes = [vec[:, k : k + 128] for k in range(0, vec.shape[1], 128)]
    lanes += [jnp.zeros((1, 128), jnp.float32)] * (16 * vec_chunks - len(lanes))
    for k in range(vec_chunks):
        part[row_chunks + k] = jnp.concatenate(lanes[16 * k : 16 * k + 16], axis=0)
    part[row_chunks + vec_chunks :] = vec_base[...]
    small[0].wait()
    small[1].wait()
    own_base[...] = (master_v[...] - base_decay * momentum_v[...]).astype(jnp.bfloat16)
    small[2].wait()
    small[3].wait()
    query_b = query_v[...].astype(jnp.bfloat16)

    pl.semaphore_wait(barrier, devices - 1)

    keep = pltpu.make_async_copy(own_base, base_all.at[me], out_sem.at[0])
    keep.start()

    def send_block(src, slot, o2, i2, recv_sem):
        remote(src, base_all.at[slot], base_send, recv_sem, o2 * INNER + i2, core).start()

    pl.when(o + 1 < outer)(lambda: send_block(own_base, me, o + 1, i, line_recv.at[o]))
    pl.when(o >= 1)(lambda: send_block(own_base, me, o - 1, i, line_recv.at[o]))
    send_block(own_base, me, o, ix, x_recv.at[o])
    send_block(own_base, me, o, iy, y_recv.at[o])

    def line_step(d):
        for side in (-1, 1):
            o2 = o + side * d

            @pl.when(jnp.logical_and(o2 >= 0, o2 < outer))
            def _(o2=o2, side=side):
                slot = o2 * INNER + i
                src = base_all.at[slot]
                wait_bytes(src, line_recv.at[o2])
                o3 = o - side
                pl.when(jnp.logical_and(o3 >= 0, o3 < outer))(
                    lambda: send_block(src, slot, o3, i, line_recv.at[o2])
                )
                send_block(src, slot, o, ix, x_recv.at[o2])
                send_block(src, slot, o, iy, y_recv.at[o2])

    def corner_step(d):
        for side in (-1, 1) if d else (1,):
            o2 = o + side * d
            by_x = d % 4 == 0 or (d % 4 == 1 and side < 0) or (d % 4 == 3 and side > 0)

            @pl.when(jnp.logical_and(o2 >= 0, o2 < outer))
            def _(o2=o2, by_x=by_x):
                slot_x, slot_y = o2 * INNER + ix, o2 * INNER + iy
                if by_x:
                    wait_bytes(base_all.at[slot_x], x_recv.at[o2])
                    send_block(base_all.at[slot_x], slot_x, o, iy, corner_recv)
                else:
                    wait_bytes(base_all.at[slot_y], y_recv.at[o2])
                    send_block(base_all.at[slot_y], slot_y, o, ix, corner_recv)

    def finish_step(d):
        for side in (-1, 1) if d else (1,):
            o2 = o + side * d
            by_x = d % 4 == 0 or (d % 4 == 1 and side < 0) or (d % 4 == 3 and side > 0)

            @pl.when(jnp.logical_and(o2 >= 0, o2 < outer))
            def _(o2=o2, by_x=by_x):
                if by_x:
                    wait_bytes(base_all.at[o2 * INNER + iy], y_recv.at[o2])
                else:
                    wait_bytes(base_all.at[o2 * INNER + ix], x_recv.at[o2])

    def send_part(k):
        mine = flat == k

        @pl.when(mine)
        def _():
            part_in[pl.ds(flat, 1)] = part[pl.ds(k, 1)]

        @pl.when(jnp.logical_not(mine))
        def _():
            remote(
                part.at[k], part_in.at[flat], part_send, part_recv, lax.rem(k, n), lax.div(k, n)
            ).start()

    def send_vec(k, carry):
        send_part(k)
        return carry

    lax.fori_loop(row_chunks, chunks, send_vec, 0)

    def row_step(b, carry):
        for copy in load(b):
            copy.wait()
        rows = pl.ds(pl.multiple_of(b * ROW_BLOCK, ROW_BLOCK), ROW_BLOCK)
        block = (
            grads_v[rows, :].astype(jnp.float32) + error_v[rows, :].astype(jnp.float32)
        ).astype(jnp.bfloat16)
        merged[rows, :] = block
        term = lax.dot_general(
            query_b, block, (((1,), (1,)), ((), ())), preferred_element_type=jnp.float32
        )
        part[pl.ds(2 * b, 1)] = term[None, :16]
        part[pl.ds(2 * b + 1, 1)] = term[None, 16:]
        send_part(2 * b)
        send_part(2 * b + 1)
        return carry

    lax.fori_loop(0, blocks, row_step, 0)
    keep_merged = pltpu.make_async_copy(merged, merged_out, out_sem.at[1])
    keep_merged.start()

    line_step(1)

    owner = flat < chunks

    @pl.when(owner)
    def _():
        wait_bytes(part_in.at[pl.ds(0, devices - 1)], part_recv)
        total[pl.ds(flat, 1)] = jnp.sum(part_in[...], axis=0)[None]

        def spread(t, carry):
            f = lax.rem(flat + t, devices)
            remote(
                total.at[flat],
                total.at[flat],
                total_send,
                total_recv,
                lax.rem(f, n),
                lax.div(f, n),
            ).start()
            return carry

        lax.fori_loop(1, devices, spread, 0)

    corner_step(0)
    if outer > 2:
        line_step(2)

    pl.when(owner)(lambda: wait_bytes(total.at[pl.ds(0, chunks - 1)], total_recv))
    pl.when(jnp.logical_not(owner))(lambda: wait_bytes(total.at[pl.ds(0, chunks)], total_recv))

    row_mean = (
        jnp.concatenate(
            [
                jnp.concatenate([total[2 * b], total[2 * b + 1]], axis=0)
                for b in range(blocks)
            ],
            axis=1,
        )
        / n
    )
    basis = jnp.dot(
        gram_v[...].T,
        row_mean,
        precision=lax.Precision.HIGHEST,
        preferred_element_type=jnp.float32,
    )
    basis_b = basis.astype(jnp.bfloat16)

    wide = columns // 4
    for c in range(4):
        term = jnp.dot(
            basis_b, merged[:, c * wide : (c + 1) * wide], preferred_element_type=jnp.float32
        )
        for r in range(4):
            k = 4 * c + r
            col_part[k] = term[8 * r : 8 * r + 8]
        for r in range(4):
            k = 4 * c + r

            @pl.when(me == k)
            def _(k=k):
                col_in[pl.ds(me, 1)] = col_part[pl.ds(k, 1)]

            @pl.when(me != k)
            def _(k=k):
                remote(
                    col_part.at[k], col_in.at[me], cpart_send, cpart_recv, k, core
                ).start()

    for d in range(3, outer):
        line_step(d)
    corner_step(1)

    high = basis_b.astype(jnp.float32)
    low = basis - high
    basis_out[...] = jnp.concatenate([high, low, high, low], axis=0).T.astype(jnp.bfloat16)
    vec_out[...] = total[row_chunks:]

    def col_owner():
        wait_bytes(col_in.at[pl.ds(0, n - 1)], cpart_recv)
        col_total[pl.ds(me, 1)] = jnp.sum(col_in[...], axis=0)[None]

        def spread(t, carry):
            remote(
                col_total.at[me],
                col_total.at[me],
                ctotal_send,
                ctotal_recv,
                lax.rem(me + t, n),
                core,
            ).start()
            return carry

        lax.fori_loop(1, n, spread, 0)

    everyone_owns = n == COL_OWNERS
    if everyone_owns:
        col_owner()
    else:
        pl.when(me < COL_OWNERS)(col_owner)

    for d in range(2, outer):
        corner_step(d)

    if everyone_owns:
        wait_bytes(col_total.at[pl.ds(0, COL_OWNERS - 1)], ctotal_recv)
    else:
        pl.when(me < COL_OWNERS)(
            lambda: wait_bytes(col_total.at[pl.ds(0, COL_OWNERS - 1)], ctotal_recv)
        )
        pl.when(me >= COL_OWNERS)(
            lambda: wait_bytes(col_total.at[pl.ds(0, COL_OWNERS)], ctotal_recv)
        )

    for c in range(4):
        col_mean = jnp.concatenate([col_total[4 * c + r] for r in range(4)], axis=0) / n
        col_high = col_mean.astype(jnp.bfloat16)
        col_low = (col_mean - col_high.astype(jnp.float32)).astype(jnp.bfloat16)
        col_out[:, c * wide : (c + 1) * wide] = jnp.concatenate(
            [col_high, col_high, col_low, col_low], axis=0
        )

    keep.wait()
    keep_merged.wait()

    @pl.when(owner)
    def _():
        wait_bytes(part.at[pl.ds(0, chunks - 1)], part_send)
        wait_bytes(part_in.at[pl.ds(0, devices - 1)], total_send)

    @pl.when(jnp.logical_not(owner))
    def _():
        wait_bytes(part.at[pl.ds(0, chunks)], part_send)

    def col_sent():
        wait_bytes(col_part.at[pl.ds(0, COL_OWNERS - 1)], cpart_send)
        wait_bytes(col_in.at[pl.ds(0, n - 1)], ctotal_send)

    if everyone_owns:
        col_sent()
    else:
        pl.when(me < COL_OWNERS)(col_sent)
        pl.when(me >= COL_OWNERS)(
            lambda: wait_bytes(col_part.at[pl.ds(0, COL_OWNERS)], cpart_send)
        )

    for d in range(outer):
        finish_step(d)
    wait_bytes(base_all.at[pl.ds(0, outer)], corner_recv)
    wait_bytes(base_all.at[pl.ds(0, 3 * outer)], base_send)
    ends = jnp.logical_or(o == 0, o == outer - 1)
    pl.when(ends)(lambda: wait_bytes(base_all.at[pl.ds(0, 1)], base_send))
    pl.when(jnp.logical_not(ends))(
        lambda: wait_bytes(base_all.at[pl.ds(0, outer + 1)], base_send)
    )


def exchange(n, cores, grads, error, query_t, gram, vec_grads, vec_base, master, momentum):
    rows_all, columns = grads.shape[1:]
    rank = query_t.shape[0]
    rows = master.shape[0]
    blocks = rows_all // ROW_BLOCK
    chunks = 2 * (blocks + vec_base.shape[0])
    wide = columns // 4
    devices = n * cores
    vmem = pl.BlockSpec(memory_space=pltpu.VMEM)
    anywhere = pl.BlockSpec(memory_space=pl.ANY)
    hbm = pl.BlockSpec(memory_space=pltpu.HBM)
    dma = pltpu.SemaphoreType.DMA
    f32, bf16 = jnp.float32, jnp.bfloat16
    return pl.pallas_call(
        functools.partial(exchange_kernel, n, cores),
        out_shape=(
            jax.ShapeDtypeStruct((rows_all, columns), bf16),
            jax.ShapeDtypeStruct((n, rows, columns), bf16),
            jax.ShapeDtypeStruct((rows_all, 4 * rank), bf16),
            jax.ShapeDtypeStruct((4 * rank, columns), bf16),
            jax.ShapeDtypeStruct((2 * vec_base.shape[0],) + vec_base.shape[1:], f32),
        ),
        in_specs=[hbm, hbm, hbm, hbm, vmem, vmem, hbm, hbm],
        out_specs=(anywhere, anywhere, vmem, vmem, vmem),
        scratch_shapes=[
            pltpu.VMEM((rows_all, columns), bf16),
            pltpu.VMEM((rows_all, columns), bf16),
            pltpu.VMEM(query_t.shape, f32),
            pltpu.VMEM(gram.shape, f32),
            pltpu.VMEM(master.shape, f32),
            pltpu.VMEM(master.shape, f32),
            pltpu.VMEM((rows_all, columns), bf16),
            pltpu.VMEM((rows, columns), bf16),
            pltpu.VMEM((chunks, 16, 128), f32),
            pltpu.VMEM((devices, 16, 128), f32),
            pltpu.VMEM((chunks, 16, 128), f32),
            pltpu.VMEM((COL_OWNERS, 8, wide), f32),
            pltpu.VMEM((n, 8, wide), f32),
            pltpu.VMEM((COL_OWNERS, 8, wide), f32),
            dma((blocks, 2)),
            dma((4,)),
            dma((2,)),
        ]
        + [dma] * 9
        + [dma((n // INNER,))] * 3
        + [dma],
        compiler_params=pltpu.CompilerParams(
            collective_id=0, has_side_effects=True, vmem_limit_bytes=VMEM_LIMIT
        ),
        cost_estimate=pl.CostEstimate(
            flops=4 * rows_all * columns * rank, bytes_accessed=14000000, transcendentals=0
        ),
        name="exchange",
    )(grads, error, query_t, gram, vec_grads, vec_base, master, momentum)


def update_kernel(
    rows_step,
    merged,
    base,
    basis,
    col,
    master,
    momentum,
    new_error,
    new_momentum,
    new_master,
    new_weights,
):
    step = pl.program_id(0)
    here = pl.ds(pl.multiple_of(step * rows_step, rows_step), rows_step)
    approx = jnp.dot(basis[here, :], col[...], preferred_element_type=jnp.float32)
    new_error[...] = (merged[...].astype(jnp.float32) - approx).astype(jnp.bfloat16)
    new_weights[...] = (base[...].astype(jnp.float32) - approx_scale * approx).astype(
        jnp.bfloat16
    )

    @pl.when(step == 0)
    def _():
        rows, rows_all = master.shape[0], basis.shape[0]
        first = lax.axis_index("dp") * rows
        shape = (rows, rows_all)
        chosen = lax.broadcasted_iota(jnp.int32, shape, 1) == first + lax.broadcasted_iota(
            jnp.int32, shape, 0
        )
        basis_rows = jnp.dot(
            chosen.astype(jnp.float32).astype(jnp.bfloat16),
            basis[...],
            preferred_element_type=jnp.float32,
        ).astype(jnp.bfloat16)
        approx_rows = jnp.dot(basis_rows, col[...], preferred_element_type=jnp.float32)
        moved = momentum_decay * momentum[...] + approx_rows
        new_momentum[...] = moved
        new_master[...] = master[...] - step_size * (approx_rows + momentum_decay * moved)


def update(merged, base, basis, col, master, momentum):
    rows_all, columns = merged.shape
    steps = 6
    rows_step = rows_all // steps
    tile = pl.BlockSpec((rows_step, columns), lambda s: (s, 0))

    def whole(x):
        return pl.BlockSpec(x.shape, lambda s: (0, 0))

    state = jax.ShapeDtypeStruct(master.shape, jnp.float32)
    return pl.pallas_call(
        functools.partial(update_kernel, rows_step),
        grid=(steps,),
        out_shape=(
            jax.ShapeDtypeStruct((1, rows_all, columns), jnp.bfloat16),
            state,
            state,
            jax.ShapeDtypeStruct((rows_all, columns), jnp.bfloat16),
        ),
        in_specs=[tile, tile, whole(basis), whole(col), whole(master), whole(momentum)],
        out_specs=(
            pl.BlockSpec((None, rows_step, columns), lambda s: (0, s, 0)),
            whole(master),
            whole(master),
            tile,
        ),
        compiler_params=pltpu.CompilerParams(vmem_limit_bytes=VMEM_LIMIT),
        name="update",
    )(merged, base, basis, col, master, momentum)


def on_device(
    n,
    cores,
    fc_grads,
    fc_error,
    query,
    gram_inverse,
    fc_master,
    fc_momentum,
    vec_grads,
    vec_master,
    vec_momentum,
):
    replica = lax.axis_index("dp")
    length, shard = vec_grads.shape[1], vec_master.shape[0]
    counts = lax.axis_index("tensor") == 0
    padded = -(-length // 2048) * 2048
    vec_base = lax.dynamic_update_slice_in_dim(
        jnp.zeros((padded,), jnp.float32),
        jnp.where(counts, vec_master - base_decay * vec_momentum, 0.0),
        replica * shard,
        0,
    ).reshape(-1, 16, 128)

    merged, base, basis, col, vec_out = exchange(
        n,
        cores,
        fc_grads,
        fc_error,
        query.T,
        gram_inverse,
        vec_grads,
        vec_base,
        fc_master,
        fc_momentum,
    )
    new_error, new_momentum, new_master, new_weights = update(
        merged, base.reshape(merged.shape), basis, col, fc_master, fc_momentum
    )
    vec_out = vec_out.reshape(2, padded)
    vec_weights = (vec_out[1, :length] - approx_scale / n * vec_out[0, :length]).astype(
        jnp.bfloat16
    )
    vec_mean = lax.dynamic_slice_in_dim(vec_out[0], replica * shard, shard, 0) / n
    vec_new_momentum = momentum_decay * vec_momentum + vec_mean
    vec_new_master = vec_master - step_size * (vec_mean + momentum_decay * vec_new_momentum)
    return (
        new_error,
        new_momentum,
        new_master,
        new_weights,
        vec_new_momentum,
        vec_new_master,
        vec_weights,
    )


def solution(mesh):
    return jax.shard_map(
        functools.partial(on_device, mesh.shape["dp"], mesh.shape["tensor"]),
        mesh=mesh,
        in_specs=(
            P("dp", None, "tensor"),
            P("dp", None, "tensor"),
            P("tensor", None),
            P(),
            P("dp", "tensor"),
            P("dp", "tensor"),
            P("dp", None),
            P("dp"),
            P("dp"),
        ),
        out_specs=(
            P("dp", None, "tensor"),
            P("dp", "tensor"),
            P("dp", "tensor"),
            P(None, "tensor"),
            P("dp"),
            P("dp"),
            P(),
        ),
        check_vma=False,
    )
```

```python
import functools

import jax
import jax.numpy as jnp
from jax import lax
from jax.experimental import pallas as pl
from jax.experimental.pallas import tpu as pltpu
from jax.sharding import PartitionSpec as P

momentum_decay = 0.9
step_size = 0.5
base_decay = step_size * momentum_decay * momentum_decay
approx_scale = step_size * (1.0 + momentum_decay)

MESH = pl.DeviceIdType.MESH
INNER = 4
ROW_BLOCK = 128
COL_OWNERS = 16
VMEM_LIMIT = 60 * 1024 * 1024


def remote(src, dst, send_sem, recv_sem, dp, core):
    return pltpu.make_async_remote_copy(
        src_ref=src,
        dst_ref=dst,
        send_sem=send_sem,
        recv_sem=recv_sem,
        device_id=(dp, core),
        device_id_type=MESH,
    )


def wait_bytes(ref, sem):
    pltpu.make_async_copy(ref, ref, sem).wait()


def exchange_kernel(
    n,
    cores,
    grads,
    error,
    query_t,
    gram,
    vec_grads,
    vec_base,
    master,
    momentum,
    merged_out,
    base_all,
    basis_out,
    col_out,
    vec_out,
    grads_v,
    error_v,
    query_v,
    gram_v,
    master_v,
    momentum_v,
    merged,
    own_base,
    part,
    part_in,
    total,
    col_part,
    col_in,
    col_total,
    load_sem,
    small_sem,
    out_sem,
    part_send,
    part_recv,
    total_send,
    total_recv,
    cpart_send,
    cpart_recv,
    ctotal_send,
    ctotal_recv,
    base_send,
    line_recv,
    x_recv,
    y_recv,
    corner_recv,
):
    rows_all, columns = merged.shape
    blocks = rows_all // ROW_BLOCK
    row_chunks = 2 * blocks
    chunks = part.shape[0]
    vec_chunks = (chunks - row_chunks) // 2
    devices = n * cores
    me, core = lax.axis_index("dp"), lax.axis_index("tensor")
    flat = core * n + me
    outer = n // INNER
    o, i = lax.div(me, INNER), lax.rem(me, INNER)
    ix = i + 1 - 2 * lax.rem(i, 2)
    iy = lax.rem(i + 2, INNER)

    small = [
        pltpu.make_async_copy(src, dst, small_sem.at[k])
        for k, (src, dst) in enumerate(
            ((master, master_v), (momentum, momentum_v), (query_t, query_v), (gram, gram_v))
        )
    ]
    for copy in small:
        copy.start()

    def load(b):
        rows = pl.ds(pl.multiple_of(b * ROW_BLOCK, ROW_BLOCK), ROW_BLOCK)
        return (
            pltpu.make_async_copy(grads.at[0, rows], grads_v.at[rows], load_sem.at[b, 0]),
            pltpu.make_async_copy(error.at[0, rows], error_v.at[rows], load_sem.at[b, 1]),
        )

    for b in range(blocks):
        for copy in load(b):
            copy.start()

    barrier = pltpu.get_barrier_semaphore()

    def greet(t, carry):
        f = lax.rem(flat + t, devices)
        pl.semaphore_signal(
            barrier, inc=1, device_id=(lax.rem(f, n), lax.div(f, n)), device_id_type=MESH
        )
        return carry

    lax.fori_loop(1, devices, greet, 0)

    vec = vec_grads[...].astype(jnp.float32) * (core == 0).astype(jnp.float32)
    lanes = [vec[:, k : k + 128] for k in range(0, vec.shape[1], 128)]
    lanes += [jnp.zeros((1, 128), jnp.float32)] * (16 * vec_chunks - len(lanes))
    for k in range(vec_chunks):
        part[row_chunks + k] = jnp.concatenate(lanes[16 * k : 16 * k + 16], axis=0)
    part[row_chunks + vec_chunks :] = vec_base[...]
    small[0].wait()
    small[1].wait()
    own_base[...] = (master_v[...] - base_decay * momentum_v[...]).astype(jnp.bfloat16)
    small[2].wait()
    small[3].wait()
    query_b = query_v[...].astype(jnp.bfloat16)

    pl.semaphore_wait(barrier, devices - 1)

    keep = pltpu.make_async_copy(own_base, base_all.at[me], out_sem.at[0])
    keep.start()

    def send_block(src, slot, o2, i2, recv_sem):
        remote(src, base_all.at[slot], base_send, recv_sem, o2 * INNER + i2, core).start()

    pl.when(o + 1 < outer)(lambda: send_block(own_base, me, o + 1, i, line_recv.at[o]))
    pl.when(o >= 1)(lambda: send_block(own_base, me, o - 1, i, line_recv.at[o]))
    send_block(own_base, me, o, ix, x_recv.at[o])
    send_block(own_base, me, o, iy, y_recv.at[o])

    def line_step(d):
        for side in (-1, 1):
            o2 = o + side * d

            @pl.when(jnp.logical_and(o2 >= 0, o2 < outer))
            def _(o2=o2, side=side):
                slot = o2 * INNER + i
                src = base_all.at[slot]
                wait_bytes(src, line_recv.at[o2])
                o3 = o - side
                pl.when(jnp.logical_and(o3 >= 0, o3 < outer))(
                    lambda: send_block(src, slot, o3, i, line_recv.at[o2])
                )
                send_block(src, slot, o, ix, x_recv.at[o2])
                send_block(src, slot, o, iy, y_recv.at[o2])

    def corner_step(d):
        for side in (-1, 1) if d else (1,):
            o2 = o + side * d
            by_x = d % 4 == 0 or (d % 4 == 1 and side < 0) or (d % 4 == 3 and side > 0)

            @pl.when(jnp.logical_and(o2 >= 0, o2 < outer))
            def _(o2=o2, by_x=by_x):
                slot_x, slot_y = o2 * INNER + ix, o2 * INNER + iy
                if by_x:
                    wait_bytes(base_all.at[slot_x], x_recv.at[o2])
                    send_block(base_all.at[slot_x], slot_x, o, iy, corner_recv)
                else:
                    wait_bytes(base_all.at[slot_y], y_recv.at[o2])
                    send_block(base_all.at[slot_y], slot_y, o, ix, corner_recv)

    def finish_step(d):
        for side in (-1, 1) if d else (1,):
            o2 = o + side * d
            by_x = d % 4 == 0 or (d % 4 == 1 and side < 0) or (d % 4 == 3 and side > 0)

            @pl.when(jnp.logical_and(o2 >= 0, o2 < outer))
            def _(o2=o2, by_x=by_x):
                if by_x:
                    wait_bytes(base_all.at[o2 * INNER + iy], y_recv.at[o2])
                else:
                    wait_bytes(base_all.at[o2 * INNER + ix], x_recv.at[o2])

    def send_part(k):
        mine = flat == k

        @pl.when(mine)
        def _():
            part_in[pl.ds(flat, 1)] = part[pl.ds(k, 1)]

        @pl.when(jnp.logical_not(mine))
        def _():
            remote(
                part.at[k], part_in.at[flat], part_send, part_recv, lax.rem(k, n), lax.div(k, n)
            ).start()

    def send_vec(k, carry):
        send_part(k)
        return carry

    lax.fori_loop(row_chunks, chunks, send_vec, 0)

    def row_step(b, carry):
        for copy in load(b):
            copy.wait()
        rows = pl.ds(pl.multiple_of(b * ROW_BLOCK, ROW_BLOCK), ROW_BLOCK)
        block = (
            grads_v[rows, :].astype(jnp.float32) + error_v[rows, :].astype(jnp.float32)
        ).astype(jnp.bfloat16)
        merged[rows, :] = block
        term = lax.dot_general(
            query_b, block, (((1,), (1,)), ((), ())), preferred_element_type=jnp.float32
        )
        part[pl.ds(2 * b, 1)] = term[None, :16]
        part[pl.ds(2 * b + 1, 1)] = term[None, 16:]
        send_part(2 * b)
        send_part(2 * b + 1)
        return carry

    lax.fori_loop(0, blocks, row_step, 0)
    keep_merged = pltpu.make_async_copy(merged, merged_out, out_sem.at[1])
    keep_merged.start()

    line_step(1)

    owner = flat < chunks

    @pl.when(owner)
    def _():
        wait_bytes(part_in.at[pl.ds(0, devices - 1)], part_recv)
        total[pl.ds(flat, 1)] = jnp.sum(part_in[...], axis=0)[None]

        def spread(t, carry):
            f = lax.rem(flat + t, devices)
            remote(
                total.at[flat],
                total.at[flat],
                total_send,
                total_recv,
                lax.rem(f, n),
                lax.div(f, n),
            ).start()
            return carry

        lax.fori_loop(1, devices, spread, 0)

    corner_step(0)
    if outer > 2:
        line_step(2)

    pl.when(owner)(lambda: wait_bytes(total.at[pl.ds(0, chunks - 1)], total_recv))
    pl.when(jnp.logical_not(owner))(lambda: wait_bytes(total.at[pl.ds(0, chunks)], total_recv))

    row_mean = (
        jnp.concatenate(
            [
                jnp.concatenate([total[2 * b], total[2 * b + 1]], axis=0)
                for b in range(blocks)
            ],
            axis=1,
        )
        / n
    )
    basis = jnp.dot(
        gram_v[...].T,
        row_mean,
        precision=lax.Precision.HIGHEST,
        preferred_element_type=jnp.float32,
    )
    basis_b = basis.astype(jnp.bfloat16)

    wide = columns // 4
    for c in range(4):
        term = jnp.dot(
            basis_b, merged[:, c * wide : (c + 1) * wide], preferred_element_type=jnp.float32
        )
        for r in range(4):
            k = 4 * c + r
            col_part[k] = term[8 * r : 8 * r + 8]
        for r in range(4):
            k = 4 * c + r

            @pl.when(me == k)
            def _(k=k):
                col_in[pl.ds(me, 1)] = col_part[pl.ds(k, 1)]

            @pl.when(me != k)
            def _(k=k):
                remote(
                    col_part.at[k], col_in.at[me], cpart_send, cpart_recv, k, core
                ).start()

    for d in range(3, outer):
        line_step(d)
    corner_step(1)

    high = basis_b.astype(jnp.float32)
    low = basis - high
    basis_out[...] = jnp.concatenate([high, low, high, low], axis=0).T.astype(jnp.bfloat16)
    vec_out[...] = total[row_chunks:]

    def col_owner():
        wait_bytes(col_in.at[pl.ds(0, n - 1)], cpart_recv)
        col_total[pl.ds(me, 1)] = jnp.sum(col_in[...], axis=0)[None]

        def spread(t, carry):
            remote(
                col_total.at[me],
                col_total.at[me],
                ctotal_send,
                ctotal_recv,
                lax.rem(me + t, n),
                core,
            ).start()
            return carry

        lax.fori_loop(1, n, spread, 0)

    everyone_owns = n == COL_OWNERS
    if everyone_owns:
        col_owner()
    else:
        pl.when(me < COL_OWNERS)(col_owner)

    for d in range(2, outer):
        corner_step(d)

    if everyone_owns:
        wait_bytes(col_total.at[pl.ds(0, COL_OWNERS - 1)], ctotal_recv)
    else:
        pl.when(me < COL_OWNERS)(
            lambda: wait_bytes(col_total.at[pl.ds(0, COL_OWNERS - 1)], ctotal_recv)
        )
        pl.when(me >= COL_OWNERS)(
            lambda: wait_bytes(col_total.at[pl.ds(0, COL_OWNERS)], ctotal_recv)
        )

    for c in range(4):
        col_mean = jnp.concatenate([col_total[4 * c + r] for r in range(4)], axis=0) / n
        col_high = col_mean.astype(jnp.bfloat16)
        col_low = (col_mean - col_high.astype(jnp.float32)).astype(jnp.bfloat16)
        col_out[:, c * wide : (c + 1) * wide] = jnp.concatenate(
            [col_high, col_high, col_low, col_low], axis=0
        )

    keep.wait()
    keep_merged.wait()

    @pl.when(owner)
    def _():
        wait_bytes(part.at[pl.ds(0, chunks - 1)], part_send)
        wait_bytes(part_in.at[pl.ds(0, devices - 1)], total_send)

    @pl.when(jnp.logical_not(owner))
    def _():
        wait_bytes(part.at[pl.ds(0, chunks)], part_send)

    def col_sent():
        wait_bytes(col_part.at[pl.ds(0, COL_OWNERS - 1)], cpart_send)
        wait_bytes(col_in.at[pl.ds(0, n - 1)], ctotal_send)

    if everyone_owns:
        col_sent()
    else:
        pl.when(me < COL_OWNERS)(col_sent)
        pl.when(me >= COL_OWNERS)(
            lambda: wait_bytes(col_part.at[pl.ds(0, COL_OWNERS)], cpart_send)
        )

    for d in range(outer):
        finish_step(d)
    wait_bytes(base_all.at[pl.ds(0, outer)], corner_recv)
    wait_bytes(base_all.at[pl.ds(0, 3 * outer)], base_send)
    ends = jnp.logical_or(o == 0, o == outer - 1)
    pl.when(ends)(lambda: wait_bytes(base_all.at[pl.ds(0, 1)], base_send))
    pl.when(jnp.logical_not(ends))(
        lambda: wait_bytes(base_all.at[pl.ds(0, outer + 1)], base_send)
    )


def exchange(n, cores, grads, error, query_t, gram, vec_grads, vec_base, master, momentum):
    rows_all, columns = grads.shape[1:]
    rank = query_t.shape[0]
    rows = master.shape[0]
    blocks = rows_all // ROW_BLOCK
    chunks = 2 * (blocks + vec_base.shape[0])
    wide = columns // 4
    devices = n * cores
    vmem = pl.BlockSpec(memory_space=pltpu.VMEM)
    anywhere = pl.BlockSpec(memory_space=pl.ANY)
    hbm = pl.BlockSpec(memory_space=pltpu.HBM)
    dma = pltpu.SemaphoreType.DMA
    f32, bf16 = jnp.float32, jnp.bfloat16
    return pl.pallas_call(
        functools.partial(exchange_kernel, n, cores),
        out_shape=(
            jax.ShapeDtypeStruct((rows_all, columns), bf16),
            jax.ShapeDtypeStruct((n, rows, columns), bf16),
            jax.ShapeDtypeStruct((rows_all, 4 * rank), bf16),
            jax.ShapeDtypeStruct((4 * rank, columns), bf16),
            jax.ShapeDtypeStruct((2 * vec_base.shape[0],) + vec_base.shape[1:], f32),
        ),
        in_specs=[hbm, hbm, hbm, hbm, vmem, vmem, hbm, hbm],
        out_specs=(anywhere, anywhere, vmem, vmem, vmem),
        scratch_shapes=[
            pltpu.VMEM((rows_all, columns), bf16),
            pltpu.VMEM((rows_all, columns), bf16),
            pltpu.VMEM(query_t.shape, f32),
            pltpu.VMEM(gram.shape, f32),
            pltpu.VMEM(master.shape, f32),
            pltpu.VMEM(master.shape, f32),
            pltpu.VMEM((rows_all, columns), bf16),
            pltpu.VMEM((rows, columns), bf16),
            pltpu.VMEM((chunks, 16, 128), f32),
            pltpu.VMEM((devices, 16, 128), f32),
            pltpu.VMEM((chunks, 16, 128), f32),
            pltpu.VMEM((COL_OWNERS, 8, wide), f32),
            pltpu.VMEM((n, 8, wide), f32),
            pltpu.VMEM((COL_OWNERS, 8, wide), f32),
            dma((blocks, 2)),
            dma((4,)),
            dma((2,)),
        ]
        + [dma] * 9
        + [dma((n // INNER,))] * 3
        + [dma],
        compiler_params=pltpu.CompilerParams(
            collective_id=0, has_side_effects=True, vmem_limit_bytes=VMEM_LIMIT
        ),
        cost_estimate=pl.CostEstimate(
            flops=4 * rows_all * columns * rank, bytes_accessed=14000000, transcendentals=0
        ),
        name="exchange",
    )(grads, error, query_t, gram, vec_grads, vec_base, master, momentum)


def update_kernel(
    rows_step,
    merged,
    base,
    basis,
    col,
    master,
    momentum,
    new_error,
    new_momentum,
    new_master,
    new_weights,
):
    step = pl.program_id(0)
    here = pl.ds(pl.multiple_of(step * rows_step, rows_step), rows_step)
    approx = jnp.dot(basis[here, :], col[...], preferred_element_type=jnp.float32)
    new_error[...] = (merged[...].astype(jnp.float32) - approx).astype(jnp.bfloat16)
    new_weights[...] = (base[...].astype(jnp.float32) - approx_scale * approx).astype(
        jnp.bfloat16
    )

    @pl.when(step == 0)
    def _():
        rows, rows_all = master.shape[0], basis.shape[0]
        first = lax.axis_index("dp") * rows
        shape = (rows, rows_all)
        chosen = lax.broadcasted_iota(jnp.int32, shape, 1) == first + lax.broadcasted_iota(
            jnp.int32, shape, 0
        )
        basis_rows = jnp.dot(
            chosen.astype(jnp.float32).astype(jnp.bfloat16),
            basis[...],
            preferred_element_type=jnp.float32,
        ).astype(jnp.bfloat16)
        approx_rows = jnp.dot(basis_rows, col[...], preferred_element_type=jnp.float32)
        moved = momentum_decay * momentum[...] + approx_rows
        new_momentum[...] = moved
        new_master[...] = master[...] - step_size * (approx_rows + momentum_decay * moved)


def update(merged, base, basis, col, master, momentum):
    rows_all, columns = merged.shape
    steps = 6
    rows_step = rows_all // steps
    tile = pl.BlockSpec((rows_step, columns), lambda s: (s, 0))

    def whole(x):
        return pl.BlockSpec(x.shape, lambda s: (0, 0))

    state = jax.ShapeDtypeStruct(master.shape, jnp.float32)
    return pl.pallas_call(
        functools.partial(update_kernel, rows_step),
        grid=(steps,),
        out_shape=(
            jax.ShapeDtypeStruct((1, rows_all, columns), jnp.bfloat16),
            state,
            state,
            jax.ShapeDtypeStruct((rows_all, columns), jnp.bfloat16),
        ),
        in_specs=[tile, tile, whole(basis), whole(col), whole(master), whole(momentum)],
        out_specs=(
            pl.BlockSpec((None, rows_step, columns), lambda s: (0, s, 0)),
            whole(master),
            whole(master),
            tile,
        ),
        compiler_params=pltpu.CompilerParams(vmem_limit_bytes=VMEM_LIMIT),
        name="update",
    )(merged, base, basis, col, master, momentum)


def on_device(
    n,
    cores,
    fc_grads,
    fc_error,
    query,
    gram_inverse,
    fc_master,
    fc_momentum,
    vec_grads,
    vec_master,
    vec_momentum,
):
    replica = lax.axis_index("dp")
    length, shard = vec_grads.shape[1], vec_master.shape[0]
    counts = lax.axis_index("tensor") == 0
    padded = -(-length // 2048) * 2048
    vec_base = lax.dynamic_update_slice_in_dim(
        jnp.zeros((padded,), jnp.float32),
        jnp.where(counts, vec_master - base_decay * vec_momentum, 0.0),
        replica * shard,
        0,
    ).reshape(-1, 16, 128)

    merged, base, basis, col, vec_out = exchange(
        n,
        cores,
        fc_grads,
        fc_error,
        query.T,
        gram_inverse,
        vec_grads,
        vec_base,
        fc_master,
        fc_momentum,
    )
    new_error, new_momentum, new_master, new_weights = update(
        merged, base.reshape(merged.shape), basis, col, fc_master, fc_momentum
    )
    vec_out = vec_out.reshape(2, padded)
    vec_weights = (vec_out[1, :length] - approx_scale / n * vec_out[0, :length]).astype(
        jnp.bfloat16
    )
    vec_mean = lax.dynamic_slice_in_dim(vec_out[0], replica * shard, shard, 0) / n
    vec_new_momentum = momentum_decay * vec_momentum + vec_mean
    vec_new_master = vec_master - step_size * (vec_mean + momentum_decay * vec_new_momentum)
    return (
        new_error,
        new_momentum,
        new_master,
        new_weights,
        vec_new_momentum,
        vec_new_master,
        vec_weights,
    )


def solution(mesh):
    return jax.shard_map(
        functools.partial(on_device, mesh.shape["dp"], mesh.shape["tensor"]),
        mesh=mesh,
        in_specs=(
            P("dp", None, "tensor"),
            P("dp", None, "tensor"),
            P("tensor", None),
            P(),
            P("dp", "tensor"),
            P("dp", "tensor"),
            P("dp", None),
            P("dp"),
            P("dp"),
        ),
        out_specs=(
            P("dp", None, "tensor"),
            P("dp", "tensor"),
            P("dp", "tensor"),
            P(None, "tensor"),
            P("dp"),
            P("dp"),
            P(),
        ),
        check_vma=False,
    )
```
